32 devices in a mesh: parts: 2 (over y), row: 8 (over z, x), col: 2 (over core).
Axes of the slice: x: 2, y: 2, z: 4, core: 2. Of those that a mesh axis runs over, the one named last changes fastest.
Arguments:
- features: bfloat16 [24576, 128], P(('parts', 'row', 'col')), parts along dimension 0, may hold values from -12 to 12
- labels: int32 [24576], P(('parts', 'row', 'col')), parts along dimension 0, may hold values from 0 to 171
- train_mask: int32 [24576], P(('parts', 'row', 'col')), parts along dimension 0, may hold values from 0 to 1, as said below
- w_one: bfloat16 [128, 256], replicated, may hold values from -0.5 to 0.5
- w_two: bfloat16 [256, 172], replicated, may hold values from -1 to 3.5
- tile_rows: int32 [16, 2, 70], P(('parts', 'row'), 'col'), parts along dimension 0, may hold values from 0 to 11, as said below
- tile_cols: int32 [16, 2, 70], P(('parts', 'row'), 'col'), parts along dimension 0, may hold values from 0 to 47, as said below
- tile_count: int32 [16, 2], P(('parts', 'row'), 'col'), parts along dimension 0, may hold values from 22 to 70, as said below
- edge_dst: int32 [16, 2, 70, 128], P(('parts', 'row'), 'col'), parts along dimension 0, may hold values from 0 to 127
- edge_src: int32 [16, 2, 70, 128], P(('parts', 'row'), 'col'), parts along dimension 0, may hold values from 0 to 127
Outputs:
- logits: float32 [24576, 172], P(('parts', 'row', 'col')), parts along dimension 0
- loss: float32 [2], P('parts'), parts along dimension 0
- grad_one: float32 [256, 256], P('parts'), parts along dimension 0
- grad_two: float32 [512, 172], P('parts'), parts along dimension 0
The draws below stay inside these ranges and needn't reach their ends.
There are 2 independent parts, one for each index of `parts`. The reference program is written for one: setup_inputs(seed, part) draws one part's arguments, and reference() takes and returns one part's arrays. A program takes and returns all parts, laid end to end along the dimension named above; an argument that names none is the same for every part. Nothing has to cross between parts.
Inputs may be any that keep to these rules, and one draw needn't show every extreme that they name: `tile_rows`: which tile of the device's block row, 12 tiles of two node blocks, a slot's destination nodes lie in. Live slots of one device name distinct tiles, listed first. The source tile of a live slot of grid row r is owned by grid row r, r + 1, r - 1, r + 2 or r - 8 / 4 (modulo 8), namely row tile_cols div 6. `tile_count`: A is symmetric. Some device fills all 70 slots. `train_mask`: the first node of every tile is a training node.
All inputs are finite; a program needn't handle non-finite values.
Results may differ from the reference program's by a relative error of at most 0.0085.
The reference program's roundings to bfloat16 on the way (of `agg_one`, `hidden`, `error_scaled`, `proj_grad` and `active_grad`) count: a program that leaves them out, or rounds other values in their place, can miss the bound.
Values sent between devices are 32-bit elements; how exact they have to be, the bound alone decides.
A program may use at most 64 MiB of HBM per device.

```python
import math
import jax
import jax.numpy as jnp
from jax import lax

F_IN = 128
HID = 256
CLASSES = 172
TILE = 128
RT = 6
E_T = 128
LIGHT_PAIRS = 2
HEAVY_PAIRS = 8
TILES_DEV = 70
NODES = 12288
N_ROW = 8
N_COL = 2


def tile_graph(key):
    key = jax.random.fold_in(key, 7)
    hot_key, pair_base, edge_key, count_key = jax.random.split(key, 4)
    hot_row = jax.random.randint(hot_key, (), 0, N_ROW, dtype=jnp.int32)
    quarter = N_ROW // 4
    full_shape = (N_ROW, 2, 4, 2, HEAVY_PAIRS)
    row_ids = jnp.arange(N_ROW, dtype=jnp.int32)[:, None, None, None, None]
    col_ids = jnp.arange(2, dtype=jnp.int32)[None, :, None, None, None]
    shift_ids = jnp.array([1, -1, quarter, -quarter], jnp.int32)[None, None, :, None, None]
    side_ids = jnp.arange(2, dtype=jnp.int32)[None, None, None, :, None]
    pick_ids = jnp.arange(HEAVY_PAIRS, dtype=jnp.int32)[None, None, None, None, :]
    other_row = (row_ids + shift_ids) % N_ROW
    low_row = jnp.minimum(row_ids, other_row)
    high_row = jnp.maximum(row_ids, other_row)
    is_low = row_ids < other_row
    col_low = jnp.where(is_low, side_ids, col_ids)
    col_high = jnp.where(is_low, col_ids, side_ids)
    combo_ids = ((low_row * N_ROW + high_row) * 2 + col_low) * 2 + col_high
    combo_ids = jnp.broadcast_to(combo_ids, (N_ROW, 2, 4, 2, 1)).reshape(-1)

    def draw_combo(combo):
        return jax.random.permutation(jax.random.fold_in(pair_base, combo), RT * RT)[:HEAVY_PAIRS].astype(jnp.int32)

    def draw_live(combo):
        return jax.random.randint(jax.random.fold_in(count_key, combo), (), LIGHT_PAIRS, HEAVY_PAIRS + 1, dtype=jnp.int32)
    chosen = jax.vmap(draw_combo)(combo_ids).reshape(full_shape)
    combo_live = jax.vmap(draw_live)(combo_ids).reshape(N_ROW, 2, 4, 2, 1)
    k_low = chosen // RT
    k_high = chosen % RT
    k_own = jnp.where(is_low, k_low, k_high)
    k_far = jnp.where(is_low, k_high, k_low)
    heavy_pair = (low_row == hot_row) | (high_row == hot_row)
    live_band = pick_ids < jnp.where(heavy_pair, HEAVY_PAIRS, combo_live)
    band_rows = jnp.broadcast_to(side_ids * RT + k_own, full_shape).reshape(N_ROW, 2, 8 * HEAVY_PAIRS)
    band_cols = jnp.broadcast_to(other_row * RT + k_far, full_shape).reshape(N_ROW, 2, 8 * HEAVY_PAIRS)
    band_live = jnp.broadcast_to(live_band, full_shape).reshape(N_ROW, 2, 8 * HEAVY_PAIRS)
    own_tiles = jnp.arange(RT, dtype=jnp.int32)[None, None, :]
    row_flat = jnp.arange(N_ROW, dtype=jnp.int32)[:, None, None]
    col_flat = jnp.arange(2, dtype=jnp.int32)[None, :, None]
    diag_rows = jnp.broadcast_to(col_flat * RT + own_tiles, (N_ROW, 2, RT))
    diag_cols = jnp.broadcast_to(row_flat * RT + own_tiles, (N_ROW, 2, RT))
    all_rows = jnp.concatenate([diag_rows, band_rows], axis=-1)
    all_cols = jnp.concatenate([diag_cols, band_cols], axis=-1)
    all_live = jnp.concatenate([jnp.ones((N_ROW, 2, RT), bool), band_live], axis=-1)
    positions = jnp.arange(TILES_DEV, dtype=jnp.int32)
    ordering = jnp.where(all_live, positions, positions + TILES_DEV)
    slot_order = jnp.argsort(ordering, axis=-1, stable=True).astype(jnp.int32)
    slot_rows = jnp.take_along_axis(all_rows, slot_order, axis=-1)
    slot_cols = jnp.take_along_axis(all_cols, slot_order, axis=-1)
    counts = jnp.sum(all_live.astype(jnp.int32), axis=-1)
    row_tile = 2 * RT * row_flat + slot_rows
    col_tile = (2 * (slot_cols // RT) + col_flat) * RT + slot_cols % RT
    tile_total = 2 * N_ROW * RT
    pair_key = jnp.minimum(row_tile, col_tile) * tile_total + jnp.maximum(row_tile, col_tile)

    def draw_pair(pair_id):
        return jax.random.randint(jax.random.fold_in(edge_key, pair_id), (2, E_T), 0, TILE, dtype=jnp.int32)
    pairs = jax.vmap(draw_pair)(pair_key.reshape(-1)).reshape(N_ROW, 2, TILES_DEV, 2, E_T)
    first = pairs[..., 0, :]
    second = pairs[..., 1, :]
    half_edges = E_T // 2
    mirror_dst = jnp.concatenate([first[..., :half_edges], second[..., :half_edges]], axis=-1)
    mirror_src = jnp.concatenate([second[..., :half_edges], first[..., :half_edges]], axis=-1)
    below = (row_tile < col_tile)[..., None]
    above = (row_tile > col_tile)[..., None]
    dst_slots = jnp.where(below, first, jnp.where(above, second, mirror_dst))
    src_slots = jnp.where(below, second, jnp.where(above, first, mirror_src))
    return (slot_rows, slot_cols, counts, dst_slots, src_slots)


def draw_tile_rows(key, part):
    return tile_graph(key)[0].astype(jnp.int32)


def draw_tile_cols(key, part):
    return tile_graph(key)[1].astype(jnp.int32)


def draw_tile_count(key, part):
    return tile_graph(key)[2].astype(jnp.int32)


def draw_edge_dst(key, part):
    return tile_graph(key)[3].astype(jnp.int32)


def draw_edge_src(key, part):
    return tile_graph(key)[4].astype(jnp.int32)


def draw_train_mask(key, part):
    key = jax.random.fold_in(key, 3)
    node_ids = jnp.arange(NODES, dtype=jnp.int32)
    threshold = 250 + 500 * node_ids // NODES
    draws = jax.random.randint(key, (NODES,), 0, 1000, dtype=jnp.int32)
    marked = (draws < threshold) | (node_ids % TILE == 0)
    return marked.astype(jnp.int32)


def draw_w_two(key, part):
    key = jax.random.fold_in(key, 5)
    spread_scale = 2.0 / math.sqrt(HID)
    normal_part = jnp.clip(jax.random.normal(key, (HID, CLASSES), jnp.float32), -6.0, 6.0)
    return jnp.clip(normal_part * spread_scale, -1.0, 3.5).astype(jnp.bfloat16)


def touch_ends(entries, rng, smallest, largest):
    dims = entries.shape
    spot = [jax.random.randint(jax.random.fold_in(rng, axis), (), 0, dims[axis]) for axis in range(len(dims))]
    entries = entries.at[tuple(spot)].set(smallest)
    longest = dims.index(max(dims))
    spot[longest] = (spot[longest] + 1) % dims[longest]
    return entries.at[tuple(spot)].set(largest)


def shard_levels(rng, dims, pieces, low, top_value):
    level = 1.0
    for position, blocks in pieces:
        steps = jax.random.uniform(jax.random.fold_in(jax.random.fold_in(rng, 6), position), (blocks,), jnp.float32, low / len(pieces), top_value / len(pieces))
        level = level * jnp.repeat(jnp.exp(steps), dims[position] // blocks).reshape((-1,) + (1,) * (len(dims) - 1 - position))
    return level


def scatter_about(own_key, dims, scale, limit, cuts=(), kind=jnp.bfloat16):
    result = scale * jax.random.normal(own_key, dims, jnp.float32)
    if cuts:
        result = result * shard_levels(own_key, dims, cuts, -0.22, 0.18)
    return jnp.clip(result, -limit, limit).astype(kind)


def setup_inputs(seed: int = 0, part: int = 0) -> dict:
    keys = jax.random.split(jax.random.key(seed), 11)
    own_keys = jax.random.split(jax.random.fold_in(keys[10], part), 11)
    return {
        "features": scatter_about(own_keys[0], (NODES, F_IN), 2.0, 12.0, ((0, 16),)),
        "labels": touch_ends(jax.random.randint(own_keys[1], (NODES,), 0, CLASSES), jax.random.fold_in(own_keys[1], 1), 0, CLASSES - 1).astype(jnp.int32),
        "train_mask": draw_train_mask(jax.random.fold_in(jax.random.fold_in(keys[10], part), 71), part),
        "w_one": scatter_about(keys[3], (F_IN, HID), F_IN ** -0.5, 0.5),
        "w_two": draw_w_two(jax.random.fold_in(keys[10], 71), part),
        "tile_rows": draw_tile_rows(jax.random.fold_in(jax.random.fold_in(keys[10], part), 71), part),
        "tile_cols": draw_tile_cols(jax.random.fold_in(jax.random.fold_in(keys[10], part), 71), part),
        "tile_count": draw_tile_count(jax.random.fold_in(jax.random.fold_in(keys[10], part), 71), part),
        "edge_dst": draw_edge_dst(jax.random.fold_in(jax.random.fold_in(keys[10], part), 71), part),
        "edge_src": draw_edge_src(jax.random.fold_in(jax.random.fold_in(keys[10], part), 71), part),
    }


def aggregate(values, graph):
    tile_rows, tile_cols, tile_count, edge_dst, edge_src = graph
    col_width = values.shape[1]
    values_f = values.astype(jnp.float32)
    col_ids = jnp.arange(N_COL, dtype=jnp.int32)[:, None]
    slot_ids = jnp.arange(TILES_DEV, dtype=jnp.int32)[None, :, None]

    def per_row(bundle):
        row_slots, col_slots, live_count, dst_slots, src_slots = bundle
        live = (slot_ids < live_count[:, None, None]).astype(jnp.float32)
        live = jnp.broadcast_to(live, dst_slots.shape).reshape(-1)
        dst_node = (row_slots[:, :, None] * TILE + dst_slots).reshape(-1).astype(jnp.int32)
        src_base = ((2 * (col_slots // RT) + col_ids) * RT + col_slots % RT) * TILE
        src_node = (src_base[:, :, None] + src_slots).reshape(-1).astype(jnp.int32)
        gathered = jnp.take(values_f, src_node, axis=0) * live[:, None]
        sums = jax.ops.segment_sum(gathered, dst_node, num_segments=2 * RT * TILE)
        counts = jax.ops.segment_sum(live, dst_node, num_segments=2 * RT * TILE)
        return sums, counts

    partials, row_sums = lax.map(per_row, (tile_rows, tile_cols, tile_count, edge_dst, edge_src))
    return partials.reshape(NODES, col_width), row_sums.reshape(NODES)


def reference(features, labels, train_mask, w_one, w_two, tile_rows, tile_cols, tile_count, edge_dst, edge_src):
    graph = (tile_rows, tile_cols, tile_count, edge_dst, edge_src)
    first_sum, row_sums = aggregate(features, graph)
    degree = 1.0 + row_sums
    agg_one = ((first_sum + features.astype(jnp.float32)) / degree[:, None]).astype(jnp.bfloat16)
    hidden = jnp.maximum(jnp.dot(agg_one, w_one, preferred_element_type=jnp.float32), 0.0).astype(jnp.bfloat16)
    projected = jnp.dot(hidden, w_two, preferred_element_type=jnp.float32)
    logit_sum, unused_sums = aggregate(projected, graph)
    logits = (logit_sum + projected) / degree[:, None]
    train_f = train_mask.astype(jnp.float32)
    train_count = jnp.sum(train_f)
    row_max = jnp.max(logits, axis=1, keepdims=True)
    log_total = row_max[:, 0] + jnp.log(jnp.sum(jnp.exp(logits - row_max), axis=1))
    onehot = (labels[:, None] == jnp.arange(CLASSES, dtype=jnp.int32)[None, :]).astype(jnp.float32)
    picked_logit = jnp.sum(onehot * logits, axis=1)
    loss_value = jnp.sum(train_f * (log_total - picked_logit)) / train_count
    probabilities = jnp.exp(logits - log_total[:, None])
    logit_grad = train_f[:, None] * (probabilities - onehot) / train_count
    error_scaled = (logit_grad / degree[:, None]).astype(jnp.bfloat16)
    back_sum, unused_back = aggregate(error_scaled, graph)
    proj_grad = (back_sum + error_scaled.astype(jnp.float32)).astype(jnp.bfloat16)
    grad_two = jnp.dot(hidden.T, proj_grad, preferred_element_type=jnp.float32)
    hidden_grad = jnp.dot(proj_grad, w_two.T, preferred_element_type=jnp.float32)
    active_grad = jnp.where(hidden > 0, hidden_grad, 0.0).astype(jnp.bfloat16)
    grad_one = jnp.dot(agg_one.T, active_grad, preferred_element_type=jnp.float32)
    return logits, loss_value.reshape(1), grad_one, grad_two
```

```python
import functools

import jax
import jax.numpy as jnp
from jax import lax
from jax.experimental import pallas as pl
from jax.experimental.pallas import tpu as pltpu
from jax.sharding import PartitionSpec as P

TILE = 128
MESH = pl.DeviceIdType.MESH
F32 = jnp.float32
BF16 = jnp.bfloat16


def ceil_to(value, unit):
    return -(-value // unit) * unit


def reduce_plan(rows, row_total):
    levels = [("col", 1)]
    bit = 1
    while bit < row_total:
        levels.append(("row", bit))
        bit *= 2
    plan = []
    for axis, bit in levels:
        halved = rows % 16 == 0
        rows = rows // 2 if halved else rows
        plan.append((axis, bit, rows, halved))
    return plan


def kernel(
    row_total, classes, plan,
    map_ref, feat_ref, w1t_ref, w2t_ref, w2_ref, lab_ref, mask_ref, esrc_ref, edst_ref,
    logits_out, g1_out, g2_out, loss_out,
    tiles, adj, x1, x2, x3, acc, rx1, rx2, rx3, hid, cnt, cnt_rx, grads, gathered, *rest,
):
    grad_rx = rest[: len(plan)]
    halo_send, halo_recv, col_send, col_recv, cnt_send, cnt_recv, sum_send, sum_recv, all_send, all_recv = rest[len(plan):]
    quarter = row_total // 4
    offsets = [0, 1, -1, quarter, -quarter]
    sources = len(offsets)
    here = lax.axis_index("row")
    col = lax.axis_index("col")
    other = 1 - col
    f_in, nodes = feat_ref.shape
    width = w2t_ref.shape[0]
    hidden_total = w1t_ref.shape[0]
    owned = nodes // TILE
    slots = esrc_ref.shape[0]

    def level_peer(axis, bit):
        if axis == "col":
            return {"col": other}
        is_set = (here // bit) % 2
        return {"row": here + bit - 2 * bit * is_set}

    def level_bit(axis, bit):
        return col if axis == "col" else (here // bit) % 2

    halo_peers = [None] + [
        {"row": lax.rem(here - off + row_total, row_total)} for off in offsets[1:]
    ]
    greet = halo_peers[1:] + [level_peer(axis, bit) for axis, bit, _, _ in plan]
    barrier = pltpu.get_barrier_semaphore()
    for peer in greet:
        pl.semaphore_signal(barrier, inc=1, device_id=peer, device_id_type=MESH)
    x1[0] = feat_ref[...]
    cnt[...] = jnp.zeros(cnt.shape, F32) + jnp.sum(mask_ref[...].astype(F32))
    pl.semaphore_wait(barrier, len(greet))

    pending = []

    def remote(src, dst, send, recv, peer):
        return pltpu.make_async_remote_copy(
            src_ref=src, dst_ref=dst, send_sem=send, recv_sem=recv,
            device_id=peer, device_id_type=MESH,
        )

    def start_halo(phase, buf):
        for p in range(sources - 1, 0, -1):
            copy = remote(
                buf.at[0], buf.at[p], halo_send.at[phase, p], halo_recv.at[phase, p], halo_peers[p]
            )
            copy.start()
            pending.append(copy)

    def wait_halo(phase, buf, p):
        remote(
            buf.at[0], buf.at[p], halo_send.at[phase, p], halo_recv.at[phase, p], {"col": other}
        ).wait_recv()

    def count_levels():
        for k, (axis, bit, _, _) in enumerate(plan):
            copy = remote(
                cnt, cnt_rx.at[k], cnt_send.at[k], cnt_recv.at[k], level_peer(axis, bit)
            )
            copy.start()
            yield
            copy.wait()
            cnt[...] += cnt_rx[k]

    counter = count_levels()
    next(counter, None)
    start_halo(0, x1)

    sub_ids = lax.broadcasted_iota(jnp.int32, (TILE, TILE), 0)
    one, zero = jnp.ones((TILE, TILE), F32), jnp.zeros((TILE, TILE), F32)

    def build(t, carry):
        src = jnp.where(sub_ids == esrc_ref[pl.ds(t, 1), :], one, zero).astype(BF16)
        dst = jnp.where(sub_ids == edst_ref[pl.ds(t, 1), :], one, zero).astype(BF16)
        tiles[t] = lax.dot_general(
            src, dst, (((1,), (1,)), ((), ())), preferred_element_type=F32
        ).astype(BF16)
        return carry

    lax.fori_loop(0, slots, build, 0, unroll=2)
    tiles[slots] = jnp.zeros((TILE, TILE), BF16)
    next(counter, None)

    def place(p, carry):
        for k in range(owned):
            for a in range(2 * owned):
                index = map_ref[(p * owned + k) * 2 * owned + a]
                adj[a // owned, p, k * TILE:(k + 1) * TILE,
                    (a % owned) * TILE:(a % owned + 1) * TILE] = tiles[index]
        return carry

    lax.fori_loop(0, sources, place, 0)
    next(counter, None)

    def aggregate(phase, buf, lhs, rows, rx):
        part = acc.at[:, 0:rows, :]
        part[...] = jnp.zeros(part.shape, F32)

        def step(p, carry):
            @pl.when(p > 0)
            def _():
                wait_halo(phase, buf, p)

            x = lhs(p)
            for d in range(2):
                part[d] += jnp.dot(x, adj[d, p], preferred_element_type=F32)
            return carry

        lax.fori_loop(0, sources - 1, step, 0)
        last = sources - 1
        wait_halo(phase, buf, last)
        x = lhs(last)
        part[other] += jnp.dot(x, adj[other, last], preferred_element_type=F32)
        copy = remote(
            part.at[other], rx, col_send.at[phase], col_recv.at[phase], {"col": other}
        )
        copy.start()
        part[col] += jnp.dot(x, adj[col, last], preferred_element_type=F32)
        copy.wait()
        return part[col] + rx[...]

    ones = jnp.ones((16, nodes), BF16)
    total = aggregate(
        0, x1, lambda p: jnp.concatenate([x1[p].astype(BF16), ones], axis=0), f_in + 16, rx1
    )
    degree = 1.0 + total[f_in:f_in + 1]
    agg = ((total[:f_in] + x1[0]) / degree).astype(BF16)
    x2[0] = agg.astype(F32)
    start_halo(1, x2)
    next(counter, None)

    def hidden_of(p):
        return jnp.maximum(
            jnp.dot(w1t_ref[...], x2[p].astype(BF16), preferred_element_type=F32), 0.0
        ).astype(BF16)

    def projected_of(p):
        return jnp.dot(w2t_ref[...], hidden_of(p), preferred_element_type=F32)

    hid[...] = hidden_of(0)
    logit_sum = aggregate(1, x2, lambda p: projected_of(p).astype(BF16), width, rx2)
    for _ in counter:
        pass
    train_count = cnt[0:1, 0:1]
    projected = jnp.dot(w2t_ref[...], hid[...], preferred_element_type=F32)
    logits = (logit_sum + projected) / degree
    logits_out[...] = logits
    class_ids = lax.broadcasted_iota(jnp.int32, (width, nodes), 0)
    masked = jnp.where(class_ids < classes, logits, -jnp.inf)
    row_max = jnp.max(masked, axis=0, keepdims=True)
    log_total = row_max + jnp.log(jnp.sum(jnp.exp(masked - row_max), axis=0, keepdims=True))
    hit = class_ids == lab_ref[...]
    train_f = mask_ref[...].astype(F32)
    probabilities = jnp.exp(masked - log_total)
    logit_grad = train_f * (probabilities - jnp.where(hit, 1.0, 0.0)) / train_count
    error = (logit_grad / degree).astype(BF16)
    x3[0] = error.astype(F32)
    start_halo(2, x3)
    picked = jnp.sum(jnp.where(hit, logits, 0.0), axis=0, keepdims=True)
    loss_local = jnp.sum(train_f * (log_total - picked))

    back_sum = aggregate(2, x3, lambda p: x3[p].astype(BF16), width, rx3)
    proj_grad = (back_sum + x3[0]).astype(BF16)
    contract_nodes = (((1,), (1,)), ((), ()))
    grad_two = lax.dot_general(proj_grad, hid[...], contract_nodes, preferred_element_type=F32)
    hidden_grad = jnp.dot(w2_ref[...], proj_grad, preferred_element_type=F32)
    active = jnp.where(hid[...].astype(F32) > 0, hidden_grad, 0.0).astype(BF16)
    grad_one = lax.dot_general(
        x2[0].astype(BF16), active, contract_nodes, preferred_element_type=F32
    )
    spots = []
    at = 0
    for grad, out in ((grad_one, g1_out), (grad_two, g2_out)):
        for lane in range(0, hidden_total, TILE):
            grads[at:at + grad.shape[0], :] = grad[:, lane:lane + TILE]
            spots.append((at, grad.shape[0], out, lane))
            at += grad.shape[0]
    grads[at:, :] = jnp.zeros((grads.shape[0] - at, TILE), F32) + loss_local

    base = 0
    bases = []
    for k, (axis, bit, rows, halved) in enumerate(plan):
        peer = level_peer(axis, bit)
        mine = level_bit(axis, bit)
        bases.append(base)
        if halved:
            keep = pl.multiple_of(base + mine * rows, 8)
            away = pl.multiple_of(base + (1 - mine) * rows, 8)
        else:
            keep = away = base
        copy = remote(
            grads.at[pl.ds(away, rows), :], grad_rx[k], sum_send.at[k], sum_recv.at[k], peer
        )
        copy.start()
        copy.wait()
        grads[pl.ds(keep, rows), :] += grad_rx[k][...]
        base = keep
    rows = plan[-1][2]
    gathered[pl.ds(base, rows), :] = grads[pl.ds(base, rows), :]
    for k in range(len(plan) - 1, -1, -1):
        axis, bit, rows, halved = plan[k]
        if not halved:
            continue
        mine = level_bit(axis, bit)
        piece = gathered.at[pl.ds(pl.multiple_of(bases[k] + mine * rows, 8), rows), :]
        copy = remote(piece, piece, all_send.at[k], all_recv.at[k], level_peer(axis, bit))
        copy.start()
        copy.wait()
    for start, count, out, lane in spots:
        out[:, lane:lane + TILE] = gathered[start:start + count, :]
    loss_out[...] = gathered[at:at + 8, :] / cnt[...]
    for copy in pending:
        copy.wait_send()


def shards(
    row_total, features, labels, train_mask, w_one, w_two, tile_rows, tile_cols, tile_count,
    edge_dst, edge_src,
):
    nodes, f_in = features.shape
    owned = nodes // TILE
    hidden_total, classes = w_two.shape
    width = ceil_to(classes, 16)
    quarter = row_total // 4
    here = lax.axis_index("row")
    offsets = [0, 1, -1, quarter, -quarter]
    sources = len(offsets)
    slot_rows, slot_cols = tile_rows[0, 0], tile_cols[0, 0]
    slots = slot_rows.shape[0]
    slot_ids = lax.iota(jnp.int32, slots)
    distance = (slot_cols // owned - here) % row_total
    position = sum(
        p * (distance == off % row_total).astype(jnp.int32) for p, off in enumerate(offsets)
    )
    spot = (position * owned + slot_cols % owned) * 2 * owned + slot_rows
    spot = jnp.where(slot_ids < tile_count[0, 0], spot, -1)
    spots_total = sources * owned * 2 * owned
    slot_map = slots + jnp.sum(
        jnp.where(lax.iota(jnp.int32, spots_total)[:, None] == spot[None, :], slot_ids - slots, 0),
        axis=1,
    )
    feat_t = features.T.astype(F32)
    w2 = jnp.pad(w_two, ((0, 0), (0, width - classes)))
    grad_rows = (f_in + width) * (hidden_total // TILE)
    grad_rows = ceil_to(grad_rows + 8, 128)
    plan = reduce_plan(grad_rows, row_total)
    levels = len(plan)
    vmem = pl.BlockSpec(memory_space=pltpu.VMEM)
    dma = pltpu.SemaphoreType.DMA
    logits_t, grad_one, grad_two_t, loss = pl.pallas_call(
        functools.partial(kernel, row_total, classes, plan),
        out_shape=(
            jax.ShapeDtypeStruct((width, nodes), F32),
            jax.ShapeDtypeStruct((f_in, hidden_total), F32),
            jax.ShapeDtypeStruct((width, hidden_total), F32),
            jax.ShapeDtypeStruct((8, TILE), F32),
        ),
        in_specs=[pl.BlockSpec(memory_space=pltpu.SMEM)] + [vmem] * 8,
        out_specs=[vmem] * 4,
        scratch_shapes=[
            pltpu.VMEM((slots + 1, TILE, TILE), BF16),
            pltpu.VMEM((2, sources, nodes, nodes), BF16),
            pltpu.VMEM((sources, f_in, nodes), F32),
            pltpu.VMEM((sources, f_in, nodes), F32),
            pltpu.VMEM((sources, width, nodes), F32),
            pltpu.VMEM((2, max(width, f_in + 16), nodes), F32),
            pltpu.VMEM((f_in + 16, nodes), F32),
            pltpu.VMEM((width, nodes), F32),
            pltpu.VMEM((width, nodes), F32),
            pltpu.VMEM((hidden_total, nodes), BF16),
            pltpu.VMEM((8, TILE), F32),
            pltpu.VMEM((levels, 8, TILE), F32),
            pltpu.VMEM((grad_rows, TILE), F32),
            pltpu.VMEM((grad_rows, TILE), F32),
        ]
        + [pltpu.VMEM((rows, TILE), F32) for _, _, rows, _ in plan]
        + [dma((3, sources)), dma((3, sources)), dma((3,)), dma((3,))]
        + [dma((levels,)) for _ in range(6)],
        compiler_params=pltpu.CompilerParams(
            collective_id=0, has_side_effects=True, vmem_limit_bytes=48 * 1024 * 1024
        ),
    )(
        slot_map, feat_t, w_one.T, w2.T, w2, labels.reshape(1, -1), train_mask.reshape(1, -1),
        edge_src[0, 0], edge_dst[0, 0],
    )
    return (
        logits_t[:classes].T,
        loss[0, :1],
        grad_one,
        grad_two_t[:classes].T,
    )


def solution(mesh):
    nodes = P(("parts", "row", "col"))
    return jax.shard_map(
        functools.partial(shards, mesh.shape["row"]),
        mesh=mesh,
        in_specs=(
            P(("parts", "row", "col"), None),
            nodes,
            nodes,
            P(),
            P(),
            P(("parts", "row"), "col", None),
            P(("parts", "row"), "col", None),
            P(("parts", "row"), "col"),
            P(("parts", "row"), "col", None, None),
            P(("parts", "row"), "col", None, None),
        ),
        out_specs=(
            P(("parts", "row", "col"), None),
            P("parts"),
            P("parts", None),
            P("parts", None),
        ),
        check_vma=False,
    )
```

```python
import functools

import jax
import jax.numpy as jnp
from jax import lax
from jax.experimental import pallas as pl
from jax.experimental.pallas import tpu as pltpu
from jax.sharding import PartitionSpec as P

TILE = 128
MESH = pl.DeviceIdType.MESH
F32 = jnp.float32
BF16 = jnp.bfloat16


def ceil_to(value, unit):
    return -(-value // unit) * unit


def pieces(rows, count):
    units = rows // 8
    cuts = [8 * (units * k // count) for k in range(count + 1)]
    return [(lo, hi - lo) for lo, hi in zip(cuts, cuts[1:])]


CHUNKS = 4


def source_offsets(row_total):
    quarter = row_total // 4
    return [0, 1, quarter, -quarter, -1]


def reduce_plan(rows, row_total):
    levels = [("col", 1)]
    bit = 1
    while bit < row_total:
        levels.append(("row", bit))
        bit *= 2
    plan = []
    for axis, bit in levels:
        halved = rows % 16 == 0
        rows = rows // 2 if halved else rows
        plan.append((axis, bit, rows, halved))
    return plan


def kernel(
    row_total, classes, plan,
    map_ref, feat_ref, w1t_ref, w2t_ref, w2_ref, lab_ref, mask_ref, esrc_ref, edst_ref,
    logits_out, g1_out, g2_out, loss_out,
    tiles, adj, x1, x2, x3, acc, rx1, rx2, rx3, hid, cnt, cnt_rx, grads, gathered, *rest,
):
    grad_rx = rest[: len(plan)]
    halo_send, halo_recv, col_send, col_recv, cnt_send, cnt_recv, sum_send, sum_recv, all_send, all_recv = rest[len(plan):]
    offsets = source_offsets(row_total)
    sources = len(offsets)
    here = lax.axis_index("row")
    sign = 1 - 2 * (here % 2)
    forwards = row_total // 4 == 2
    wraps = []
    for off in offsets[2:4]:
        lap = (here + sign * off + row_total) // row_total - 1
        wraps.append(lap * lap)
    third = 2 + wraps[0]
    fourth = 3 - wraps[0] + wraps[1]
    fifth = 4 - wraps[1]
    col = lax.axis_index("col")
    other = 1 - col
    f_in, nodes = feat_ref.shape
    width = w2t_ref.shape[0]
    hidden_total = w1t_ref.shape[0]
    owned = nodes // TILE
    slots = esrc_ref.shape[0]

    def level_peer(axis, bit):
        if axis == "col":
            return {"col": other}
        is_set = (here // bit) % 2
        return {"row": here + bit - 2 * bit * is_set}

    def level_bit(axis, bit):
        return col if axis == "col" else (here // bit) % 2

    def row_at(off):
        return {"row": lax.rem(here + sign * off + row_total, row_total)}

    quarter_flip = (row_total // 4) % 2
    near, far = (offsets[2], offsets[3]) if quarter_flip else (offsets[3], offsets[2])
    halo_peers = [None, row_at(1), row_at(near), row_at(far), row_at(-1)]
    greet = halo_peers[1:] + [level_peer(axis, bit) for axis, bit, _, _ in plan]
    barrier = pltpu.get_barrier_semaphore()
    for peer in greet:
        pl.semaphore_signal(barrier, inc=1, device_id=peer, device_id_type=MESH)
    x1[0] = feat_ref[...]
    cnt[...] = jnp.zeros(cnt.shape, F32) + jnp.sum(mask_ref[...].astype(F32))
    pl.semaphore_wait(barrier, len(greet))

    pending = []

    def remote(src, dst, send, recv, peer):
        return pltpu.make_async_remote_copy(
            src_ref=src, dst_ref=dst, send_sem=send, recv_sem=recv,
            device_id=peer, device_id_type=MESH,
        )

    def halo_copy(phase, buf, source, p, k, peer):
        lo, rows = pieces(buf.shape[1], CHUNKS)[k]
        return remote(
            buf.at[source, pl.ds(lo, rows), :], buf.at[p, pl.ds(lo, rows), :],
            halo_send.at[phase, p, k], halo_recv.at[phase, p, k], peer,
        )

    def start_halo(phase, buf):
        for p in (2, 1, 3) if forwards else (2, 1, 3, 4):
            for k in range(CHUNKS):
                copy = halo_copy(phase, buf, 0, p, k, halo_peers[p])
                copy.start()
                pending.append(copy)
        if forwards:
            pending.extend(
                halo_copy(phase, buf, 2, 4, k, halo_peers[1]) for k in range(CHUNKS)
            )

    def wait_halo(phase, buf, p):
        for k in range(CHUNKS):
            halo_copy(phase, buf, 0, p, k, {"col": other}).wait_recv()
            if forwards:
                @pl.when(p == 2)
                def _():
                    halo_copy(phase, buf, 2, 4, k, halo_peers[1]).start()

    def count_levels():
        for k, (axis, bit, _, _) in enumerate(plan):
            copy = remote(
                cnt, cnt_rx.at[k], cnt_send.at[k], cnt_recv.at[k], level_peer(axis, bit)
            )
            copy.start()
            yield
            copy.wait()
            cnt[...] += cnt_rx[k]

    counter = count_levels()
    next(counter, None)
    start_halo(0, x1)

    sub_ids = lax.broadcasted_iota(jnp.int32, (TILE, TILE), 0)
    one, zero = jnp.ones((TILE, TILE), F32), jnp.zeros((TILE, TILE), F32)

    def build(t, carry):
        src = jnp.where(sub_ids == esrc_ref[pl.ds(t, 1), :], one, zero).astype(BF16)
        dst = jnp.where(sub_ids == edst_ref[pl.ds(t, 1), :], one, zero).astype(BF16)
        tiles[t] = lax.dot_general(
            src, dst, (((1,), (1,)), ((), ())), preferred_element_type=F32
        ).astype(BF16)
        return carry

    lax.fori_loop(0, slots, build, 0, unroll=2)
    tiles[slots] = jnp.zeros((TILE, TILE), BF16)
    next(counter, None)

    def place(p, carry):
        for k in range(owned):
            for a in range(2 * owned):
                index = map_ref[(p * owned + k) * 2 * owned + a]
                adj[a // owned, p, k * TILE:(k + 1) * TILE,
                    (a % owned) * TILE:(a % owned + 1) * TILE] = tiles[index]
        return carry

    lax.fori_loop(0, sources, place, 0)
    next(counter, None)

    def aggregate(phase, buf, lhs, rows, rx):
        part = acc.at[:, 0:rows, :]
        part[...] = jnp.zeros(part.shape, F32)

        def step(i, carry):
            p = jnp.where(i == 2, third, jnp.where(i == 3, fourth, i))

            @pl.when(i > 0)
            def _():
                wait_halo(phase, buf, p)

            x = lhs(p)
            for d in range(2):
                part[d] += jnp.dot(x, adj[d, p], preferred_element_type=F32)
            return carry

        lax.fori_loop(0, sources - 1, step, 0)
        last = fifth
        wait_halo(phase, buf, last)
        x = lhs(last)
        part[other] += jnp.dot(x, adj[other, last], preferred_element_type=F32)
        copy = remote(
            part.at[other], rx, col_send.at[phase], col_recv.at[phase], {"col": other}
        )
        copy.start()
        part[col] += jnp.dot(x, adj[col, last], preferred_element_type=F32)
        copy.wait()
        return part[col] + rx[...]

    ones = jnp.ones((16, nodes), BF16)
    total = aggregate(
        0, x1, lambda p: jnp.concatenate([x1[p].astype(BF16), ones], axis=0), f_in + 16, rx1
    )
    degree = 1.0 + total[f_in:f_in + 1]
    agg = ((total[:f_in] + x1[0]) / degree).astype(BF16)
    x2[0] = agg.astype(F32)
    start_halo(1, x2)
    next(counter, None)

    def hidden_of(p):
        return jnp.maximum(
            jnp.dot(w1t_ref[...], x2[p].astype(BF16), preferred_element_type=F32), 0.0
        ).astype(BF16)

    def projected_of(p):
        return jnp.dot(w2t_ref[...], hidden_of(p), preferred_element_type=F32)

    hid[...] = hidden_of(0)
    logit_sum = aggregate(1, x2, lambda p: projected_of(p).astype(BF16), width, rx2)
    for _ in counter:
        pass
    train_count = cnt[0:1, 0:1]
    projected = jnp.dot(w2t_ref[...], hid[...], preferred_element_type=F32)
    logits = (logit_sum + projected) / degree
    logits_out[...] = logits
    class_ids = lax.broadcasted_iota(jnp.int32, (width, nodes), 0)
    masked = jnp.where(class_ids < classes, logits, -jnp.inf)
    row_max = jnp.max(masked, axis=0, keepdims=True)
    log_total = row_max + jnp.log(jnp.sum(jnp.exp(masked - row_max), axis=0, keepdims=True))
    hit = class_ids == lab_ref[...]
    train_f = mask_ref[...].astype(F32)
    probabilities = jnp.exp(masked - log_total)
    logit_grad = train_f * (probabilities - jnp.where(hit, 1.0, 0.0)) / train_count
    error = (logit_grad / degree).astype(BF16)
    x3[0] = error.astype(F32)
    start_halo(2, x3)
    picked = jnp.sum(jnp.where(hit, logits, 0.0), axis=0, keepdims=True)
    loss_local = jnp.sum(train_f * (log_total - picked))

    back_sum = aggregate(2, x3, lambda p: x3[p].astype(BF16), width, rx3)
    proj_grad = (back_sum + x3[0]).astype(BF16)
    contract_nodes = (((1,), (1,)), ((), ()))
    grad_two = lax.dot_general(proj_grad, hid[...], contract_nodes, preferred_element_type=F32)
    hidden_grad = jnp.dot(w2_ref[...], proj_grad, preferred_element_type=F32)
    active = jnp.where(hid[...].astype(F32) > 0, hidden_grad, 0.0).astype(BF16)
    grad_one = lax.dot_general(
        x2[0].astype(BF16), active, contract_nodes, preferred_element_type=F32
    )
    spots = []
    at = 0
    for grad, out in ((grad_one, g1_out), (grad_two, g2_out)):
        for lane in range(0, hidden_total, TILE):
            grads[at:at + grad.shape[0], :] = grad[:, lane:lane + TILE]
            spots.append((at, grad.shape[0], out, lane))
            at += grad.shape[0]
    grads[at:, :] = jnp.zeros((grads.shape[0] - at, TILE), F32) + loss_local

    base = 0
    bases = []
    for k, (axis, bit, rows, halved) in enumerate(plan):
        peer = level_peer(axis, bit)
        mine = level_bit(axis, bit)
        bases.append(base)
        if halved:
            keep = pl.multiple_of(base + mine * rows, 8)
            away = pl.multiple_of(base + (1 - mine) * rows, 8)
        else:
            keep = away = base
        copy = remote(
            grads.at[pl.ds(away, rows), :], grad_rx[k], sum_send.at[k], sum_recv.at[k], peer
        )
        copy.start()
        copy.wait()
        grads[pl.ds(keep, rows), :] += grad_rx[k][...]
        base = keep
    rows = plan[-1][2]
    gathered[pl.ds(base, rows), :] = grads[pl.ds(base, rows), :]
    for k in range(len(plan) - 1, -1, -1):
        axis, bit, rows, halved = plan[k]
        if not halved:
            continue
        mine = level_bit(axis, bit)
        piece = gathered.at[pl.ds(pl.multiple_of(bases[k] + mine * rows, 8), rows), :]
        copy = remote(piece, piece, all_send.at[k], all_recv.at[k], level_peer(axis, bit))
        copy.start()
        copy.wait()
    for start, count, out, lane in spots:
        out[:, lane:lane + TILE] = gathered[start:start + count, :]
    loss_out[...] = gathered[at:at + 8, :] / cnt[...]
    for copy in pending:
        copy.wait_send()


def shards(
    row_total, features, labels, train_mask, w_one, w_two, tile_rows, tile_cols, tile_count,
    edge_dst, edge_src,
):
    nodes, f_in = features.shape
    owned = nodes // TILE
    hidden_total, classes = w_two.shape
    width = ceil_to(classes, 16)
    here = lax.axis_index("row")
    sign = 1 - 2 * (here % 2)
    offsets = source_offsets(row_total)
    sources = len(offsets)
    slot_rows, slot_cols = tile_rows[0, 0], tile_cols[0, 0]
    slots = slot_rows.shape[0]
    slot_ids = lax.iota(jnp.int32, slots)
    distance = (slot_cols // owned - here) % row_total
    position = sum(
        p * (distance == (sign * off) % row_total).astype(jnp.int32) for p, off in enumerate(offsets)
    )
    spot = (position * owned + slot_cols % owned) * 2 * owned + slot_rows
    spot = jnp.where(slot_ids < tile_count[0, 0], spot, -1)
    spots_total = sources * owned * 2 * owned
    slot_map = slots + jnp.sum(
        jnp.where(lax.iota(jnp.int32, spots_total)[:, None] == spot[None, :], slot_ids - slots, 0),
        axis=1,
    )
    feat_t = features.T.astype(F32)
    w2 = jnp.pad(w_two, ((0, 0), (0, width - classes)))
    grad_rows = (f_in + width) * (hidden_total // TILE)
    grad_rows = ceil_to(grad_rows + 8, 128)
    plan = reduce_plan(grad_rows, row_total)
    levels = len(plan)
    vmem = pl.BlockSpec(memory_space=pltpu.VMEM)
    dma = pltpu.SemaphoreType.DMA
    logits_t, grad_one, grad_two_t, loss = pl.pallas_call(
        functools.partial(kernel, row_total, classes, plan),
        out_shape=(
            jax.ShapeDtypeStruct((width, nodes), F32),
            jax.ShapeDtypeStruct((f_in, hidden_total), F32),
            jax.ShapeDtypeStruct((width, hidden_total), F32),
            jax.ShapeDtypeStruct((8, TILE), F32),
        ),
        in_specs=[pl.BlockSpec(memory_space=pltpu.SMEM)] + [vmem] * 8,
        out_specs=[vmem] * 4,
        scratch_shapes=[
            pltpu.VMEM((slots + 1, TILE, TILE), BF16),
            pltpu.VMEM((2, sources, nodes, nodes), BF16),
            pltpu.VMEM((sources, f_in, nodes), F32),
            pltpu.VMEM((sources, f_in, nodes), F32),
            pltpu.VMEM((sources, width, nodes), F32),
            pltpu.VMEM((2, max(width, f_in + 16), nodes), F32),
            pltpu.VMEM((f_in + 16, nodes), F32),
            pltpu.VMEM((width, nodes), F32),
            pltpu.VMEM((width, nodes), F32),
            pltpu.VMEM((hidden_total, nodes), BF16),
            pltpu.VMEM((8, TILE), F32),
            pltpu.VMEM((levels, 8, TILE), F32),
            pltpu.VMEM((grad_rows, TILE), F32),
            pltpu.VMEM((grad_rows, TILE), F32),
        ]
        + [pltpu.VMEM((rows, TILE), F32) for _, _, rows, _ in plan]
        + [dma((3, sources, CHUNKS)), dma((3, sources, CHUNKS)), dma((3,)), dma((3,))]
        + [dma((levels,)) for _ in range(6)],
        compiler_params=pltpu.CompilerParams(
            collective_id=0, has_side_effects=True, vmem_limit_bytes=48 * 1024 * 1024
        ),
    )(
        slot_map, feat_t, w_one.T, w2.T, w2, labels.reshape(1, -1), train_mask.reshape(1, -1),
        edge_src[0, 0], edge_dst[0, 0],
    )
    return (
        logits_t[:classes].T,
        loss[0, :1],
        grad_one,
        grad_two_t[:classes].T,
    )


def solution(mesh):
    nodes = P(("parts", "row", "col"))
    return jax.shard_map(
        functools.partial(shards, mesh.shape["row"]),
        mesh=mesh,
        in_specs=(
            P(("parts", "row", "col"), None),
            nodes,
            nodes,
            P(),
            P(),
            P(("parts", "row"), "col", None),
            P(("parts", "row"), "col", None),
            P(("parts", "row"), "col"),
            P(("parts", "row"), "col", None, None),
            P(("parts", "row"), "col", None, None),
        ),
        out_specs=(
            P(("parts", "row", "col"), None),
            P("parts"),
            P("parts", None),
            P("parts", None),
        ),
        check_vma=False,
    )
```

```python
import functools

import jax
import jax.numpy as jnp
from jax import lax
from jax.experimental import pallas as pl
from jax.experimental.pallas import tpu as pltpu
from jax.sharding import PartitionSpec as P

TILE = 128
MESH = pl.DeviceIdType.MESH
F32 = jnp.float32
BF16 = jnp.bfloat16


def ceil_to(value, unit):
    return -(-value // unit) * unit


def pieces(rows, count):
    units = rows // 8
    cuts = [8 * (units * k // count) for k in range(count + 1)]
    return [(lo, hi - lo) for lo, hi in zip(cuts, cuts[1:])]


CHUNKS = 4


def source_offsets(row_total):
    quarter = row_total // 4
    return [0, 1, quarter, -quarter, -1]


def reduce_plan(rows, row_total):
    levels = [("col", 1)]
    bit = 1
    while bit < row_total:
        levels.append(("row", bit))
        bit *= 2
    plan = []
    for axis, bit in levels:
        halved = rows % 16 == 0
        rows = rows // 2 if halved else rows
        plan.append((axis, bit, rows, halved))
    return plan


def kernel(
    row_total, classes, plan,
    map_ref, feat_ref, w1t_ref, w2t_ref, w2_ref, lab_ref, mask_ref, esrc_ref, edst_ref,
    logits_out, g1_out, g2_out, loss_out,
    tiles, adj, x1, x2, x3, acc, rx1, rx2, rx3, hid, cnt, cnt_rx, grads, gathered, *rest,
):
    buffers = 2 if row_total <= 8 else len(plan)
    grad_rx = rest[:buffers]
    halo_send, halo_recv, col_send, col_recv, cnt_send, cnt_recv, sum_send, sum_recv, all_send, all_recv = rest[buffers:]
    offsets = source_offsets(row_total)
    sources = len(offsets)
    here = lax.axis_index("row")
    sign = 1 - 2 * (here % 2)
    forwards = row_total // 4 == 2
    col = lax.axis_index("col")
    other = 1 - col
    f_in, nodes = feat_ref.shape
    width = w2t_ref.shape[0]
    hidden_total = w1t_ref.shape[0]
    owned = nodes // TILE
    slots = esrc_ref.shape[0]

    def level_peer(axis, bit):
        if axis == "col":
            return {"col": other}
        is_set = (here // bit) % 2
        return {"row": here + bit - 2 * bit * is_set}

    def level_bit(axis, bit):
        return col if axis == "col" else (here // bit) % 2

    def row_at(off):
        return {"row": lax.rem(here + sign * off + row_total, row_total)}

    quarter_flip = (row_total // 4) % 2
    near, far = (offsets[2], offsets[3]) if quarter_flip else (offsets[3], offsets[2])
    halo_peers = [None, row_at(1), row_at(near), row_at(far), row_at(-1)]
    direct = row_total <= 8
    everyone = [
        {"row": lax.rem(here + by, row_total), "col": col if side == 0 else other}
        for by in range(row_total) for side in range(2)
    ][1:] if direct else []
    if direct:
        greet = everyone
    else:
        greet = halo_peers[1:] + [level_peer(axis, bit) for axis, bit, _, _ in plan]
    barrier = pltpu.get_barrier_semaphore()
    for peer in greet:
        pl.semaphore_signal(barrier, inc=1, device_id=peer, device_id_type=MESH)
    x1[0] = feat_ref[...]
    cnt[...] = jnp.zeros(cnt.shape, F32) + jnp.sum(mask_ref[...].astype(F32))
    pl.semaphore_wait(barrier, len(greet))

    pending = []

    def remote(src, dst, send, recv, peer):
        return pltpu.make_async_remote_copy(
            src_ref=src, dst_ref=dst, send_sem=send, recv_sem=recv,
            device_id=peer, device_id_type=MESH,
        )

    def halo_copy(phase, buf, source, p, k, peer):
        lo, rows = pieces(buf.shape[1], CHUNKS)[k]
        return remote(
            buf.at[source, pl.ds(lo, rows), :], buf.at[p, pl.ds(lo, rows), :],
            halo_send.at[phase, p, k], halo_recv.at[phase, p, k], peer,
        )

    def start_halo(phase, buf, sources=(2, 1) if forwards else (2, 1, 3, 4)):
        for p in sources:
            for k in range(CHUNKS):
                copy = halo_copy(phase, buf, 0, p, k, halo_peers[p])
                copy.start()
                pending.append(copy)

    def forward_halo(phase, buf):
        for k in range(CHUNKS):
            halo_copy(phase, buf, 0, 2, k, halo_peers[2]).wait_recv()
            copy = halo_copy(phase, buf, 2, 4, k, halo_peers[1])
            copy.start()
            pending.append(copy)
        for copy in pending[-3 * CHUNKS:-2 * CHUNKS]:
            copy.wait_send()
        del pending[-3 * CHUNKS:-2 * CHUNKS]
        start_halo(phase, buf, (3,))

    def wait_halo(phase, buf, p):
        for k in range(CHUNKS):
            halo_copy(phase, buf, 0, p, k, {"col": other}).wait_recv()

    def count_levels():
        for k, (axis, bit, _, _) in enumerate(plan):
            copy = remote(
                cnt, cnt_rx.at[k], cnt_send.at[k], cnt_recv.at[k], level_peer(axis, bit)
            )
            copy.start()
            yield
            copy.wait()
            cnt[...] += cnt_rx[k]

    counter = iter(()) if direct else count_levels()
    start_halo(0, x1)
    if direct:
        counts = [
            remote(cnt, cnt_rx.at[k], cnt_send.at[k], cnt_recv.at[k], peer)
            for k, peer in enumerate(everyone)
        ]
        for copy in counts:
            copy.start()
    next(counter, None)

    sub_ids = lax.broadcasted_iota(jnp.int32, (TILE, TILE), 0)
    one, zero = jnp.ones((TILE, TILE), F32), jnp.zeros((TILE, TILE), F32)

    def build(t, carry):
        src = jnp.where(sub_ids == esrc_ref[pl.ds(t, 1), :], one, zero).astype(BF16)
        dst = jnp.where(sub_ids == edst_ref[pl.ds(t, 1), :], one, zero).astype(BF16)
        tiles[t] = lax.dot_general(
            src, dst, (((1,), (1,)), ((), ())), preferred_element_type=F32
        ).astype(BF16)
        return carry

    lax.fori_loop(0, slots, build, 0, unroll=2)
    tiles[slots] = jnp.zeros((TILE, TILE), BF16)
    next(counter, None)

    def place(p, carry):
        for k in range(owned):
            for a in range(2 * owned):
                index = map_ref[(p * owned + k) * 2 * owned + a]
                adj[a // owned, p, k * TILE:(k + 1) * TILE,
                    (a % owned) * TILE:(a % owned + 1) * TILE] = tiles[index]
        return carry

    lax.fori_loop(0, sources, place, 0)
    next(counter, None)

    def aggregate(phase, buf, lhs, rows, rx):
        part = acc.at[:, 0:rows, :]
        part[...] = jnp.zeros(part.shape, F32)

        def step(p, carry):
            if forwards:
                pl.when(p != 2)(functools.partial(wait_halo, phase, buf, p))
            else:
                wait_halo(phase, buf, p)

            add(p)
            return carry

        def add(p):
            x = lhs(p)
            for d in range(2):
                part[d] += jnp.dot(x, adj[d, p], preferred_element_type=F32)

        add(0)
        if forwards:
            forward_halo(phase, buf)
        order = (0, 1, 2, 4, 3) if forwards else (0, 1, 2, 3, 4)
        last = order[-1]
        lax.fori_loop(
            0, 3, lambda i, carry: step(i + 1 + (i // 2) * (order[3] - 3), carry), 0
        )
        wait_halo(phase, buf, last)
        x = lhs(last)
        part[other] += jnp.dot(x, adj[other, last], preferred_element_type=F32)
        copy = remote(
            part.at[other], rx, col_send.at[phase], col_recv.at[phase], {"col": other}
        )
        copy.start()
        part[col] += jnp.dot(x, adj[col, last], preferred_element_type=F32)
        copy.wait()
        return part[col] + rx[...]

    ones = jnp.ones((16, nodes), BF16)
    total = aggregate(
        0, x1, lambda p: jnp.concatenate([x1[p].astype(BF16), ones], axis=0), f_in + 16, rx1
    )
    degree = 1.0 + total[f_in:f_in + 1]
    agg = ((total[:f_in] + x1[0]) / degree).astype(BF16)
    x2[0] = agg.astype(F32)
    start_halo(1, x2)
    next(counter, None)

    def hidden_of(p):
        return jnp.maximum(
            jnp.dot(w1t_ref[...], x2[p].astype(BF16), preferred_element_type=F32), 0.0
        ).astype(BF16)

    def projected_of(p):
        return jnp.dot(w2t_ref[...], hidden_of(p), preferred_element_type=F32)

    hid[...] = hidden_of(0)
    logit_sum = aggregate(1, x2, lambda p: projected_of(p).astype(BF16), width, rx2)
    for _ in counter:
        pass
    if direct:
        for copy in counts:
            copy.wait()
        cnt[...] += jnp.sum(cnt_rx[...], axis=0)
    train_count = cnt[0:1, 0:1]
    projected = jnp.dot(w2t_ref[...], hid[...], preferred_element_type=F32)
    logits = (logit_sum + projected) / degree
    logits_out[...] = logits
    class_ids = lax.broadcasted_iota(jnp.int32, (width, nodes), 0)
    masked = jnp.where(class_ids < classes, logits, -jnp.inf)
    row_max = jnp.max(masked, axis=0, keepdims=True)
    log_total = row_max + jnp.log(jnp.sum(jnp.exp(masked - row_max), axis=0, keepdims=True))
    hit = class_ids == lab_ref[...]
    train_f = mask_ref[...].astype(F32)
    probabilities = jnp.exp(masked - log_total)
    logit_grad = train_f * (probabilities - jnp.where(hit, 1.0, 0.0)) / train_count
    error = (logit_grad / degree).astype(BF16)
    x3[0] = error.astype(F32)
    start_halo(2, x3)
    picked = jnp.sum(jnp.where(hit, logits, 0.0), axis=0, keepdims=True)
    loss_local = jnp.sum(train_f * (log_total - picked))

    back_sum = aggregate(2, x3, lambda p: x3[p].astype(BF16), width, rx3)
    proj_grad = (back_sum + x3[0]).astype(BF16)
    contract_nodes = (((1,), (1,)), ((), ()))
    grad_two = lax.dot_general(proj_grad, hid[...], contract_nodes, preferred_element_type=F32)
    hidden_grad = jnp.dot(w2_ref[...], proj_grad, preferred_element_type=F32)
    active = jnp.where(hid[...].astype(F32) > 0, hidden_grad, 0.0).astype(BF16)
    grad_one = lax.dot_general(
        x2[0].astype(BF16), active, contract_nodes, preferred_element_type=F32
    )
    spots = []
    at = 0
    for grad, out in ((grad_one, g1_out), (grad_two, g2_out)):
        for lane in range(0, hidden_total, TILE):
            grads[at:at + grad.shape[0], :] = grad[:, lane:lane + TILE]
            spots.append((at, grad.shape[0], out, lane))
            at += grad.shape[0]
    grads[at:, :] = jnp.zeros((grads.shape[0] - at, TILE), F32) + loss_local

    if direct:
        half = grads.shape[0] // 2
        rows = half // row_total
        mine = pl.multiple_of(col * half, 8)
        away = pl.multiple_of(other * half, 8)
        copy = remote(
            grads.at[pl.ds(away, half), :], grad_rx[0], sum_send.at[0], sum_recv.at[0],
            {"col": other},
        )
        copy.start()
        copy.wait()
        grads[pl.ds(mine, half), :] += grad_rx[0][...]
        hops = sorted(range(1, row_total), key=lambda by: -min(by, row_total - by))
        piece = pl.multiple_of(mine + here * rows, 8)
        copies = []
        for by in hops:
            there = lax.rem(here + by, row_total)
            copies.append(remote(
                grads.at[pl.ds(pl.multiple_of(mine + there * rows, 8), rows), :],
                grad_rx[1].at[by - 1], sum_send.at[by], sum_recv.at[by], {"row": there},
            ))
            copies[-1].start()
        for copy in copies:
            copy.wait()
        gathered[pl.ds(piece, rows), :] = grads[pl.ds(piece, rows), :] + jnp.sum(
            grad_rx[1][...], axis=0
        )
        copies = []
        for by in hops:
            there = lax.rem(here + by, row_total)
            spot = gathered.at[pl.ds(piece, rows), :]
            copies.append(
                remote(spot, spot, all_send.at[by], all_recv.at[by], {"row": there})
            )
            copies[-1].start()
        for copy in copies:
            copy.wait()
        spot = gathered.at[pl.ds(mine, half), :]
        copy = remote(spot, spot, all_send.at[0], all_recv.at[0], {"col": other})
        copy.start()
        copy.wait()
    else:
        base = 0
        bases = []
        for k, (axis, bit, rows, halved) in enumerate(plan):
            peer = level_peer(axis, bit)
            mine = level_bit(axis, bit)
            bases.append(base)
            if halved:
                keep = pl.multiple_of(base + mine * rows, 8)
                away = pl.multiple_of(base + (1 - mine) * rows, 8)
            else:
                keep = away = base
            copy = remote(
                grads.at[pl.ds(away, rows), :], grad_rx[k], sum_send.at[k], sum_recv.at[k], peer
            )
            copy.start()
            copy.wait()
            grads[pl.ds(keep, rows), :] += grad_rx[k][...]
            base = keep
        rows = plan[-1][2]
        gathered[pl.ds(base, rows), :] = grads[pl.ds(base, rows), :]
        for k in range(len(plan) - 1, -1, -1):
            axis, bit, rows, halved = plan[k]
            if not halved:
                continue
            mine = level_bit(axis, bit)
            piece = gathered.at[pl.ds(pl.multiple_of(bases[k] + mine * rows, 8), rows), :]
            copy = remote(piece, piece, all_send.at[k], all_recv.at[k], level_peer(axis, bit))
            copy.start()
            copy.wait()
    for start, count, out, lane in spots:
        out[:, lane:lane + TILE] = gathered[start:start + count, :]
    loss_out[...] = gathered[at:at + 8, :] / cnt[...]
    for copy in pending:
        copy.wait_send()


def shards(
    row_total, features, labels, train_mask, w_one, w_two, tile_rows, tile_cols, tile_count,
    edge_dst, edge_src,
):
    nodes, f_in = features.shape
    owned = nodes // TILE
    hidden_total, classes = w_two.shape
    width = ceil_to(classes, 16)
    here = lax.axis_index("row")
    sign = 1 - 2 * (here % 2)
    offsets = source_offsets(row_total)
    sources = len(offsets)
    slot_rows, slot_cols = tile_rows[0, 0], tile_cols[0, 0]
    slots = slot_rows.shape[0]
    slot_ids = lax.iota(jnp.int32, slots)
    distance = (slot_cols // owned - here) % row_total
    position = sum(
        p * (distance == (sign * off) % row_total).astype(jnp.int32) for p, off in enumerate(offsets)
    )
    spot = (position * owned + slot_cols % owned) * 2 * owned + slot_rows
    spot = jnp.where(slot_ids < tile_count[0, 0], spot, -1)
    spots_total = sources * owned * 2 * owned
    slot_map = slots + jnp.sum(
        jnp.where(lax.iota(jnp.int32, spots_total)[:, None] == spot[None, :], slot_ids - slots, 0),
        axis=1,
    )
    feat_t = features.T.astype(F32)
    w2 = jnp.pad(w_two, ((0, 0), (0, width - classes)))
    grad_rows = (f_in + width) * (hidden_total // TILE)
    grad_rows = ceil_to(grad_rows + 8, 128)
    plan = reduce_plan(grad_rows, row_total)
    direct = row_total <= 8
    levels = 2 * row_total if direct else len(plan)
    if direct:
        half = grad_rows // 2
        grad_buffers = [(half, TILE), (row_total - 1, half // row_total, TILE)]
    else:
        grad_buffers = [(rows, TILE) for _, _, rows, _ in plan]
    vmem = pl.BlockSpec(memory_space=pltpu.VMEM)
    dma = pltpu.SemaphoreType.DMA
    logits_t, grad_one, grad_two_t, loss = pl.pallas_call(
        functools.partial(kernel, row_total, classes, plan),
        out_shape=(
            jax.ShapeDtypeStruct((width, nodes), F32),
            jax.ShapeDtypeStruct((f_in, hidden_total), F32),
            jax.ShapeDtypeStruct((width, hidden_total), F32),
            jax.ShapeDtypeStruct((8, TILE), F32),
        ),
        in_specs=[pl.BlockSpec(memory_space=pltpu.SMEM)] + [vmem] * 8,
        out_specs=[vmem] * 4,
        scratch_shapes=[
            pltpu.VMEM((slots + 1, TILE, TILE), BF16),
            pltpu.VMEM((2, sources, nodes, nodes), BF16),
            pltpu.VMEM((sources, f_in, nodes), F32),
            pltpu.VMEM((sources, f_in, nodes), F32),
            pltpu.VMEM((sources, width, nodes), F32),
            pltpu.VMEM((2, max(width, f_in + 16), nodes), F32),
            pltpu.VMEM((f_in + 16, nodes), F32),
            pltpu.VMEM((width, nodes), F32),
            pltpu.VMEM((width, nodes), F32),
            pltpu.VMEM((hidden_total, nodes), BF16),
            pltpu.VMEM((8, TILE), F32),
            pltpu.VMEM((levels - 1 if direct else levels, 8, TILE), F32),
            pltpu.VMEM((grad_rows, TILE), F32),
            pltpu.VMEM((grad_rows, TILE), F32),
        ]
        + [pltpu.VMEM(shape, F32) for shape in grad_buffers]
        + [dma((3, sources, CHUNKS)), dma((3, sources, CHUNKS)), dma((3,)), dma((3,))]
        + [dma((levels,)) for _ in range(6)],
        compiler_params=pltpu.CompilerParams(
            collective_id=0, has_side_effects=True, vmem_limit_bytes=48 * 1024 * 1024
        ),
    )(
        slot_map, feat_t, w_one.T, w2.T, w2, labels.reshape(1, -1), train_mask.reshape(1, -1),
        edge_src[0, 0], edge_dst[0, 0],
    )
    return (
        logits_t[:classes].T,
        loss[0, :1],
        grad_one,
        grad_two_t[:classes].T,
    )


def solution(mesh):
    nodes = P(("parts", "row", "col"))
    return jax.shard_map(
        functools.partial(shards, mesh.shape["row"]),
        mesh=mesh,
        in_specs=(
            P(("parts", "row", "col"), None),
            nodes,
            nodes,
            P(),
            P(),
            P(("parts", "row"), "col", None),
            P(("parts", "row"), "col", None),
            P(("parts", "row"), "col"),
            P(("parts", "row"), "col", None, None),
            P(("parts", "row"), "col", None, None),
        ),
        out_specs=(
            P(("parts", "row", "col"), None),
            P("parts"),
            P("parts", None),
            P("parts", None),
        ),
        check_vma=False,
    )
```

```python
import functools

import jax
import jax.numpy as jnp
from jax import lax
from jax.experimental import pallas as pl
from jax.experimental.pallas import tpu as pltpu
from jax.sharding import PartitionSpec as P

TILE = 128
MESH = pl.DeviceIdType.MESH
F32 = jnp.float32
BF16 = jnp.bfloat16


def ceil_to(value, unit):
    return -(-value // unit) * unit


def pieces(rows, count):
    units = rows // 8
    cuts = [8 * (units * k // count) for k in range(count + 1)]
    return [(lo, hi - lo) for lo, hi in zip(cuts, cuts[1:])]


CHUNKS = 4


def source_offsets(row_total):
    quarter = row_total // 4
    return [0, 1, quarter, -quarter, -1]


def reduce_plan(rows, row_total):
    levels = [("col", 1)]
    bit = 1
    while bit < row_total:
        levels.append(("row", bit))
        bit *= 2
    plan = []
    for axis, bit in levels:
        halved = rows % 16 == 0
        rows = rows // 2 if halved else rows
        plan.append((axis, bit, rows, halved))
    return plan


def kernel(
    row_total, classes, plan,
    map_ref, feat_ref, w1t_ref, w2t_ref, w2_ref, lab_ref, mask_ref, esrc_ref, edst_ref,
    logits_out, g1_out, g2_out, loss_out,
    tiles, adj, x1, x2, x3, acc, rx1, rx2, rx3, hid, cnt, cnt_rx, grads, gathered, *rest,
):
    buffers = 2 if row_total <= 8 else len(plan)
    grad_rx = rest[:buffers]
    halo_send, halo_recv, col_send, col_recv, cnt_send, cnt_recv, sum_send, sum_recv, all_send, all_recv = rest[buffers:]
    offsets = source_offsets(row_total)
    sources = len(offsets)
    here = lax.axis_index("row")
    sign = 1 - 2 * (here % 2)
    forwards = row_total // 4 == 2
    col = lax.axis_index("col")
    other = 1 - col
    f_in, nodes = feat_ref.shape
    width = w2t_ref.shape[0]
    hidden_total = w1t_ref.shape[0]
    owned = nodes // TILE
    slots = esrc_ref.shape[0]

    def level_peer(axis, bit):
        if axis == "col":
            return {"col": other}
        is_set = (here // bit) % 2
        return {"row": here + bit - 2 * bit * is_set}

    def level_bit(axis, bit):
        return col if axis == "col" else (here // bit) % 2

    def row_at(off):
        return {"row": lax.rem(here + sign * off + row_total, row_total)}

    quarter_flip = (row_total // 4) % 2
    near, far = (offsets[2], offsets[3]) if quarter_flip else (offsets[3], offsets[2])
    halo_peers = [None, row_at(1), row_at(near), row_at(far), row_at(-1)]
    direct = row_total <= 8
    everyone = [
        {"row": lax.rem(here + by, row_total), "col": col if side == 0 else other}
        for by in range(row_total) for side in range(2)
    ][1:] if direct else []
    if direct:
        greet = everyone
    else:
        greet = halo_peers[1:] + [level_peer(axis, bit) for axis, bit, _, _ in plan]
    barrier = pltpu.get_barrier_semaphore()
    for peer in greet:
        pl.semaphore_signal(barrier, inc=1, device_id=peer, device_id_type=MESH)
    x1[0] = feat_ref[...]
    cnt[...] = jnp.zeros(cnt.shape, F32) + jnp.sum(mask_ref[...].astype(F32))
    pl.semaphore_wait(barrier, len(greet))

    pending = []

    def remote(src, dst, send, recv, peer):
        return pltpu.make_async_remote_copy(
            src_ref=src, dst_ref=dst, send_sem=send, recv_sem=recv,
            device_id=peer, device_id_type=MESH,
        )

    def halo_copy(phase, buf, source, p, k, peer):
        lo, rows = pieces(buf.shape[1], CHUNKS)[k]
        return remote(
            buf.at[source, pl.ds(lo, rows), :], buf.at[p, pl.ds(lo, rows), :],
            halo_send.at[phase, p, k], halo_recv.at[phase, p, k], peer,
        )

    def start_halo(phase, buf, sources=(2, 1) if forwards else (2, 1, 3, 4)):
        for p in sources:
            for k in range(CHUNKS):
                copy = halo_copy(phase, buf, 0, p, k, halo_peers[p])
                copy.start()
                pending.append(copy)

    def forward_halo(phase, buf):
        for k in range(CHUNKS):
            halo_copy(phase, buf, 0, 2, k, halo_peers[2]).wait_recv()
            copy = halo_copy(phase, buf, 2, 4, k, halo_peers[1])
            copy.start()
            pending.append(copy)
        for copy in pending[-3 * CHUNKS:-2 * CHUNKS]:
            copy.wait_send()
        del pending[-3 * CHUNKS:-2 * CHUNKS]
        start_halo(phase, buf, (3,))

    def wait_halo(phase, buf, p):
        for k in range(CHUNKS):
            halo_copy(phase, buf, 0, p, k, {"col": other}).wait_recv()

    def count_levels():
        for k, (axis, bit, _, _) in enumerate(plan):
            copy = remote(
                cnt, cnt_rx.at[k], cnt_send.at[k], cnt_recv.at[k], level_peer(axis, bit)
            )
            copy.start()
            yield
            copy.wait()
            cnt[...] += cnt_rx[k]

    counter = iter(()) if direct else count_levels()
    start_halo(0, x1)
    if direct:
        counts = [
            remote(cnt, cnt_rx.at[k], cnt_send.at[k], cnt_recv.at[k], peer)
            for k, peer in enumerate(everyone)
        ]
        for copy in counts:
            copy.start()
    next(counter, None)

    sub_ids = lax.broadcasted_iota(jnp.int32, (TILE, TILE), 0)
    one, zero = jnp.ones((TILE, TILE), F32), jnp.zeros((TILE, TILE), F32)

    def build(t, carry):
        src = jnp.where(sub_ids == esrc_ref[pl.ds(t, 1), :], one, zero).astype(BF16)
        dst = jnp.where(sub_ids == edst_ref[pl.ds(t, 1), :], one, zero).astype(BF16)
        tiles[t] = lax.dot_general(
            src, dst, (((1,), (1,)), ((), ())), preferred_element_type=F32
        ).astype(BF16)
        return carry

    lax.fori_loop(0, slots, build, 0, unroll=2)
    tiles[slots] = jnp.zeros((TILE, TILE), BF16)
    if forwards:
        forward_halo(0, x1)
    next(counter, None)

    def place(p, carry):
        for k in range(owned):
            for a in range(2 * owned):
                index = map_ref[(p * owned + k) * 2 * owned + a]
                adj[a // owned, p, k * TILE:(k + 1) * TILE,
                    (a % owned) * TILE:(a % owned + 1) * TILE] = tiles[index]
        return carry

    lax.fori_loop(0, sources, place, 0)
    next(counter, None)

    def aggregate(phase, buf, lhs, rows, rx):
        part = acc.at[:, 0:rows, :]
        part[...] = jnp.zeros(part.shape, F32)

        def step(p, carry):
            if forwards:
                pl.when(p != 2)(functools.partial(wait_halo, phase, buf, p))
            else:
                wait_halo(phase, buf, p)

            add(p)
            return carry

        def add(p):
            x = lhs(p)
            for d in range(2):
                part[d] += jnp.dot(x, adj[d, p], preferred_element_type=F32)

        add(0)
        if forwards and phase > 0:
            forward_halo(phase, buf)
        order = (0, 1, 2, 4, 3) if forwards else (0, 1, 2, 3, 4)
        last = order[-1]
        lax.fori_loop(
            0, 3, lambda i, carry: step(i + 1 + (i // 2) * (order[3] - 3), carry), 0
        )
        wait_halo(phase, buf, last)
        x = lhs(last)
        part[other] += jnp.dot(x, adj[other, last], preferred_element_type=F32)
        copy = remote(
            part.at[other], rx, col_send.at[phase], col_recv.at[phase], {"col": other}
        )
        copy.start()
        part[col] += jnp.dot(x, adj[col, last], preferred_element_type=F32)
        copy.wait()
        return part[col] + rx[...]

    ones = jnp.ones((16, nodes), BF16)
    total = aggregate(
        0, x1, lambda p: jnp.concatenate([x1[p].astype(BF16), ones], axis=0), f_in + 16, rx1
    )
    degree = 1.0 + total[f_in:f_in + 1]
    agg = ((total[:f_in] + x1[0]) / degree).astype(BF16)
    x2[0] = agg.astype(F32)
    start_halo(1, x2)
    next(counter, None)

    def hidden_of(p):
        return jnp.maximum(
            jnp.dot(w1t_ref[...], x2[p].astype(BF16), preferred_element_type=F32), 0.0
        ).astype(BF16)

    def projected_of(p):
        return jnp.dot(w2t_ref[...], hidden_of(p), preferred_element_type=F32)

    hid[...] = hidden_of(0)
    x3[0] = jnp.dot(w2t_ref[...], hid[...], preferred_element_type=F32)
    logit_sum = aggregate(1, x2, lambda p: projected_of(p).astype(BF16), width, rx2)
    for _ in counter:
        pass
    if direct:
        for copy in counts:
            copy.wait()
        cnt[...] += jnp.sum(cnt_rx[...], axis=0)
    train_count = cnt[0:1, 0:1]
    logits = (logit_sum + x3[0]) / degree
    logits_out[...] = logits
    class_ids = lax.broadcasted_iota(jnp.int32, (width, nodes), 0)
    masked = jnp.where(class_ids < classes, logits, -jnp.inf)
    row_max = jnp.max(masked, axis=0, keepdims=True)
    log_total = row_max + jnp.log(jnp.sum(jnp.exp(masked - row_max), axis=0, keepdims=True))
    hit = class_ids == lab_ref[...]
    train_f = mask_ref[...].astype(F32)
    probabilities = jnp.exp(masked - log_total)
    logit_grad = train_f * (probabilities - jnp.where(hit, 1.0, 0.0)) / train_count
    error = (logit_grad / degree).astype(BF16)
    x3[0] = error.astype(F32)
    start_halo(2, x3)
    picked = jnp.sum(jnp.where(hit, logits, 0.0), axis=0, keepdims=True)
    loss_local = jnp.sum(train_f * (log_total - picked))

    back_sum = aggregate(2, x3, lambda p: x3[p].astype(BF16), width, rx3)
    proj_grad = (back_sum + x3[0]).astype(BF16)
    contract_nodes = (((1,), (1,)), ((), ()))
    grad_two = lax.dot_general(proj_grad, hid[...], contract_nodes, preferred_element_type=F32)
    hidden_grad = jnp.dot(w2_ref[...], proj_grad, preferred_element_type=F32)
    active = jnp.where(hid[...].astype(F32) > 0, hidden_grad, 0.0).astype(BF16)
    grad_one = lax.dot_general(
        x2[0].astype(BF16), active, contract_nodes, preferred_element_type=F32
    )
    spots = []
    at = 0
    for grad, out in ((grad_one, g1_out), (grad_two, g2_out)):
        for lane in range(0, hidden_total, TILE):
            grads[at:at + grad.shape[0], :] = grad[:, lane:lane + TILE]
            spots.append((at, grad.shape[0], out, lane))
            at += grad.shape[0]
    grads[at:, :] = jnp.zeros((grads.shape[0] - at, TILE), F32) + loss_local

    if direct:
        half = grads.shape[0] // 2
        rows = half // row_total
        mine = pl.multiple_of(col * half, 8)
        away = pl.multiple_of(other * half, 8)
        copy = remote(
            grads.at[pl.ds(away, half), :], grad_rx[0], sum_send.at[0], sum_recv.at[0],
            {"col": other},
        )
        copy.start()
        copy.wait()
        grads[pl.ds(mine, half), :] += grad_rx[0][...]
        hops = sorted(range(1, row_total), key=lambda by: -min(by, row_total - by))
        piece = pl.multiple_of(mine + here * rows, 8)
        copies = []
        for by in hops:
            there = lax.rem(here + by, row_total)
            copies.append(remote(
                grads.at[pl.ds(pl.multiple_of(mine + there * rows, 8), rows), :],
                grad_rx[1].at[by - 1], sum_send.at[by], sum_recv.at[by], {"row": there},
            ))
            copies[-1].start()
        for copy in copies:
            copy.wait()
        gathered[pl.ds(piece, rows), :] = grads[pl.ds(piece, rows), :] + jnp.sum(
            grad_rx[1][...], axis=0
        )
        copies = []
        for by in hops:
            there = lax.rem(here + by, row_total)
            spot = gathered.at[pl.ds(piece, rows), :]
            copies.append(
                remote(spot, spot, all_send.at[by], all_recv.at[by], {"row": there})
            )
            copies[-1].start()
        for copy in copies:
            copy.wait()
        spot = gathered.at[pl.ds(mine, half), :]
        copy = remote(spot, spot, all_send.at[0], all_recv.at[0], {"col": other})
        copy.start()
        copy.wait()
    else:
        base = 0
        bases = []
        for k, (axis, bit, rows, halved) in enumerate(plan):
            peer = level_peer(axis, bit)
            mine = level_bit(axis, bit)
            bases.append(base)
            if halved:
                keep = pl.multiple_of(base + mine * rows, 8)
                away = pl.multiple_of(base + (1 - mine) * rows, 8)
            else:
                keep = away = base
            copy = remote(
                grads.at[pl.ds(away, rows), :], grad_rx[k], sum_send.at[k], sum_recv.at[k], peer
            )
            copy.start()
            copy.wait()
            grads[pl.ds(keep, rows), :] += grad_rx[k][...]
            base = keep
        rows = plan[-1][2]
        gathered[pl.ds(base, rows), :] = grads[pl.ds(base, rows), :]
        for k in range(len(plan) - 1, -1, -1):
            axis, bit, rows, halved = plan[k]
            if not halved:
                continue
            mine = level_bit(axis, bit)
            piece = gathered.at[pl.ds(pl.multiple_of(bases[k] + mine * rows, 8), rows), :]
            copy = remote(piece, piece, all_send.at[k], all_recv.at[k], level_peer(axis, bit))
            copy.start()
            copy.wait()
    for start, count, out, lane in spots:
        out[:, lane:lane + TILE] = gathered[start:start + count, :]
    loss_out[...] = gathered[at:at + 8, :] / cnt[...]
    for copy in pending:
        copy.wait_send()


def shards(
    row_total, features, labels, train_mask, w_one, w_two, tile_rows, tile_cols, tile_count,
    edge_dst, edge_src,
):
    nodes, f_in = features.shape
    owned = nodes // TILE
    hidden_total, classes = w_two.shape
    width = ceil_to(classes, 16)
    here = lax.axis_index("row")
    sign = 1 - 2 * (here % 2)
    offsets = source_offsets(row_total)
    sources = len(offsets)
    slot_rows, slot_cols = tile_rows[0, 0], tile_cols[0, 0]
    slots = slot_rows.shape[0]
    slot_ids = lax.iota(jnp.int32, slots)
    distance = (slot_cols // owned - here) % row_total
    position = sum(
        p * (distance == (sign * off) % row_total).astype(jnp.int32) for p, off in enumerate(offsets)
    )
    spot = (position * owned + slot_cols % owned) * 2 * owned + slot_rows
    spot = jnp.where(slot_ids < tile_count[0, 0], spot, -1)
    spots_total = sources * owned * 2 * owned
    slot_map = slots + jnp.sum(
        jnp.where(lax.iota(jnp.int32, spots_total)[:, None] == spot[None, :], slot_ids - slots, 0),
        axis=1,
    )
    feat_t = features.T.astype(F32)
    w2 = jnp.pad(w_two, ((0, 0), (0, width - classes)))
    grad_rows = (f_in + width) * (hidden_total // TILE)
    grad_rows = ceil_to(grad_rows + 8, 128)
    plan = reduce_plan(grad_rows, row_total)
    direct = row_total <= 8
    levels = 2 * row_total if direct else len(plan)
    if direct:
        half = grad_rows // 2
        grad_buffers = [(half, TILE), (row_total - 1, half // row_total, TILE)]
    else:
        grad_buffers = [(rows, TILE) for _, _, rows, _ in plan]
    vmem = pl.BlockSpec(memory_space=pltpu.VMEM)
    dma = pltpu.SemaphoreType.DMA
    logits_t, grad_one, grad_two_t, loss = pl.pallas_call(
        functools.partial(kernel, row_total, classes, plan),
        out_shape=(
            jax.ShapeDtypeStruct((width, nodes), F32),
            jax.ShapeDtypeStruct((f_in, hidden_total), F32),
            jax.ShapeDtypeStruct((width, hidden_total), F32),
            jax.ShapeDtypeStruct((8, TILE), F32),
        ),
        in_specs=[pl.BlockSpec(memory_space=pltpu.SMEM)] + [vmem] * 8,
        out_specs=[vmem] * 4,
        scratch_shapes=[
            pltpu.VMEM((slots + 1, TILE, TILE), BF16),
            pltpu.VMEM((2, sources, nodes, nodes), BF16),
            pltpu.VMEM((sources, f_in, nodes), F32),
            pltpu.VMEM((sources, f_in, nodes), F32),
            pltpu.VMEM((sources, width, nodes), F32),
            pltpu.VMEM((2, max(width, f_in + 16), nodes), F32),
            pltpu.VMEM((f_in + 16, nodes), F32),
            pltpu.VMEM((width, nodes), F32),
            pltpu.VMEM((width, nodes), F32),
            pltpu.VMEM((hidden_total, nodes), BF16),
            pltpu.VMEM((8, TILE), F32),
            pltpu.VMEM((levels - 1 if direct else levels, 8, TILE), F32),
            pltpu.VMEM((grad_rows, TILE), F32),
            pltpu.VMEM((grad_rows, TILE), F32),
        ]
        + [pltpu.VMEM(shape, F32) for shape in grad_buffers]
        + [dma((3, sources, CHUNKS)), dma((3, sources, CHUNKS)), dma((3,)), dma((3,))]
        + [dma((levels,)) for _ in range(6)],
        compiler_params=pltpu.CompilerParams(
            collective_id=0, has_side_effects=True, vmem_limit_bytes=48 * 1024 * 1024
        ),
    )(
        slot_map, feat_t, w_one.T, w2.T, w2, labels.reshape(1, -1), train_mask.reshape(1, -1),
        edge_src[0, 0], edge_dst[0, 0],
    )
    return (
        logits_t[:classes].T,
        loss[0, :1],
        grad_one,
        grad_two_t[:classes].T,
    )


def solution(mesh):
    nodes = P(("parts", "row", "col"))
    return jax.shard_map(
        functools.partial(shards, mesh.shape["row"]),
        mesh=mesh,
        in_specs=(
            P(("parts", "row", "col"), None),
            nodes,
            nodes,
            P(),
            P(),
            P(("parts", "row"), "col", None),
            P(("parts", "row"), "col", None),
            P(("parts", "row"), "col"),
            P(("parts", "row"), "col", None, None),
            P(("parts", "row"), "col", None, None),
        ),
        out_specs=(
            P(("parts", "row", "col"), None),
            P("parts"),
            P("parts", None),
            P("parts", None),
        ),
        check_vma=False,
    )
```
